256 devices in a mesh: gx: 4 (over y), gy: 4 (over x), gz: 16 (over z, core).
Axes of the slice: x: 4, y: 4, z: 8, core: 2. Of those that a mesh axis runs over, the one named last changes fastest.
Arguments:
- positions: float32 [3, 131072], P(None, ('gx', 'gy', 'gz')), may hold values from 0 to 8
- features: float32 [131072, 128], P(('gx', 'gy', 'gz')), may hold values from -6 to 6
- species: int32 [131072], P(('gx', 'gy', 'gz')), may hold values from 0 to 88
- species_embed: float32 [89, 128], replicated, may hold values from -3 to 3
- w_charge: float32 [128, 128], replicated, may hold values from -0.5 to 0.5
- wave_vectors: float32 [3, 1024], replicated, may hold values from -8 to 8
- wave_filter: float32 [1024, 128], replicated, may hold values from 0.02 to 0.2
- radial_decay: float32 [128], replicated, may hold values from 0.2 to 2
- w_edge: float32 [128, 128], replicated, may hold values from -0.5 to 0.5
- w_out: float32 [128, 128], replicated, may hold values from -0.5 to 0.5
- neighbour_index: int32 [131072, 16], P(('gx', 'gy', 'gz')), may hold values from 0 to 895
- edge_count: int32 [131072], P(('gx', 'gy', 'gz')), may hold values from 1 to 16
- edge_length: float32 [131072, 16], P(('gx', 'gy', 'gz')), may hold values from 0.8 to 4.5
- face_rows: int32 [1536, 64], P(('gx', 'gy', 'gz')), may hold values from 0 to 511
- cotangent: float32 [131072, 128], P(('gx', 'gy', 'gz')), may hold values from -6 to 6
Outputs:
- update: float32 [131072, 128], P(('gx', 'gy', 'gz'))
- grad_features: float32 [131072, 128], P(('gx', 'gy', 'gz'))
The draws below stay inside these ranges and needn't reach their ends.
Inputs may be any that keep to these rules, and one draw needn't show every extreme that they name: `neighbour_index`: indexes the rows of the atom's brick's extended array: its 512 atoms, then six blocks of 64 received rows; slots at or past edge_count are unused. `face_rows`: rows 6 b to 6 b + 5 hold brick b's atoms (indices within the brick) sent to the lower and upper neighbours along gx, gy, gz in turn.
All inputs are finite; a program needn't handle non-finite values.
Results may differ from the reference program's by a relative error of at most 0.0003.
Values sent between devices are 32-bit elements; how exact they have to be, the bound alone decides.
A program may use at most 64 MiB of HBM per device.

```python
import math
import jax
import jax.numpy as jnp
import numpy as np
from jax import lax

C = 128
K = 1024
SPEC = 89
MAXNB = 16
A_DEV = 512
HALO = 64
ATOMS = 131072
N_GX = 4
N_GY = 4
N_GZ = 16
DEVICES = 256


def draw_edge_count(key, part):
    key = jax.random.fold_in(key, 7)
    first, second = jax.random.split(key)
    bricks = ATOMS // A_DEV
    ceiling = jax.random.randint(first, (bricks,), MAXNB // 2, MAXNB + 1)
    counts = jax.random.randint(second, (ATOMS,), 1, MAXNB + 1)
    counts = jnp.minimum(counts, jnp.repeat(ceiling, A_DEV, total_repeat_length=ATOMS))
    counts = counts.at[0].set(MAXNB)
    return counts.astype(jnp.int32)


def set_ends(entries, key, low, largest):
    place = [jax.random.randint(jax.random.fold_in(key, axis), (), 0, length) for axis, length in enumerate(entries.shape)]
    longest = entries.shape.index(max(entries.shape))
    next_to = place[:longest] + [(place[longest] + 1) % entries.shape[longest]] + place[longest + 1:]
    return entries.at[tuple(place)].set(low).at[tuple(next_to)].set(largest)


def block_scale(own_key, dims, pieces, low, largest):
    factor_of = 1.0
    for position, parts in pieces:
        steps = jax.random.uniform(jax.random.fold_in(jax.random.fold_in(own_key, 6), position), (parts,), jnp.float32, low / len(pieces), largest / len(pieces))
        factor_of = factor_of * jnp.repeat(jnp.exp(steps), dims[position] // parts).reshape((-1,) + (1,) * (len(dims) - 1 - position))
    return factor_of


def rank_table(count, slope):
    loads = [(1 << 20) // math.isqrt(rank ** slope) + 1 for rank in range(1, count + 1)]
    scale = 1 + sum(loads) // (1 << 30)
    return np.cumsum(np.array([max(1, weight // scale) for weight in loads]))


def ranked_ids(rng, shape, number_of, lean):
    listing = rank_table(number_of, lean)
    lot = jax.random.randint(jax.random.fold_in(rng, 1), shape, 0, int(listing[number_of - 1]))
    grade = jnp.searchsorted(jnp.asarray(listing, jnp.int32), lot, side="right")
    return jax.random.permutation(jax.random.fold_in(rng, 2), number_of)[grade].astype(jnp.int32)


def bell_draw(stream_key, shape, deviation, bound, cuts=(), kind=jnp.bfloat16):
    entries = deviation * jax.random.normal(stream_key, shape, jnp.float32)
    if cuts:
        entries = entries * block_scale(stream_key, shape, cuts, -0.22, 0.18)
    return jnp.clip(entries, -bound, bound).astype(kind)


def setup_inputs(seed: int = 0) -> dict:
    key_list = jax.random.split(jax.random.key(seed), 16)
    positions = jnp.clip(8.0 * jax.random.uniform(key_list[0], (3, ATOMS), jnp.float32) ** block_scale(key_list[0], (3, ATOMS), ((1, 256),), -0.2, 0.2), 0.0, 8.0)
    features = bell_draw(key_list[1], (ATOMS, C), 1.0, 6.0, ((0, 256),), jnp.float32)
    species = set_ends(ranked_ids(key_list[2], (ATOMS,), SPEC, 2), jax.random.fold_in(key_list[2], 3), 0, SPEC - 1).astype(jnp.int32)
    species_embed = bell_draw(key_list[3], (SPEC, C), 0.5, 3.0, (), jnp.float32)
    w_charge = bell_draw(key_list[4], (C, C), C ** -0.5, 0.5, (), jnp.float32)
    wave_vectors = bell_draw(key_list[5], (3, K), 2.0, 8.0, (), jnp.float32)
    wave_filter = jnp.clip(jnp.exp(jax.random.uniform(key_list[6], (K, C), jnp.float32, math.log(0.02), math.log(0.2))), 0.02, 0.2)
    radial_decay = jnp.clip(jnp.exp(jax.random.uniform(key_list[7], (C,), jnp.float32, math.log(0.2), math.log(2.0))), 0.2, 2.0)
    w_edge = bell_draw(key_list[8], (C, C), C ** -0.5, 0.5, (), jnp.float32)
    w_out = bell_draw(key_list[9], (C, C), C ** -0.5, 0.5, (), jnp.float32)
    neighbour_index = set_ends(jax.random.randint(key_list[10], (ATOMS, MAXNB), 0, A_DEV + 6 * HALO), jax.random.fold_in(key_list[10], 1), 0, (A_DEV + 6 * HALO) - 1).astype(jnp.int32)
    edge_count = draw_edge_count(jax.random.fold_in(key_list[15], 71), 0)
    edge_length = jnp.clip(0.8 + 3.7 * jax.random.uniform(key_list[12], (ATOMS, MAXNB), jnp.float32) ** block_scale(key_list[12], (ATOMS, MAXNB), ((0, 256),), -0.2, 0.2), 0.8, 4.5)
    face_rows = set_ends(jax.random.randint(key_list[13], (6 * DEVICES, HALO), 0, A_DEV), jax.random.fold_in(key_list[13], 1), 0, A_DEV - 1).astype(jnp.int32)
    cotangent = bell_draw(key_list[14], (ATOMS, C), 1.0, 6.0, ((0, 256),), jnp.float32)
    return dict(positions=positions, features=features, species=species, species_embed=species_embed, w_charge=w_charge, wave_vectors=wave_vectors, wave_filter=wave_filter, radial_decay=radial_decay, w_edge=w_edge, w_out=w_out, neighbour_index=neighbour_index, edge_count=edge_count, edge_length=edge_length, face_rows=face_rows, cotangent=cotangent)


cutoff = 5.0
highest = lax.Precision.HIGHEST


def radial(edge_length, edge_count, radial_decay):
    scaled = edge_length / cutoff
    envelope = (1.0 - scaled * scaled) ** 2
    active = lax.broadcasted_iota(jnp.int32, edge_length.shape, 1) < edge_count[:, None]
    weight = jnp.where(active, envelope, 0.0)
    return weight[:, :, None] * jnp.exp(-radial_decay[None, None, :] * edge_length[:, :, None])


def trig_tables(wave_vectors, block_positions):
    phases = lax.dot_general(wave_vectors, block_positions, (((0,), (0,)), ((), ())), precision=highest)
    return jnp.cos(phases), jnp.sin(phases)


def contract(table, values):
    return lax.dot_general(table, values, (((0,), (0,)), ((), ())), precision=highest)


def neighbours(device, axis_id):
    extent = (N_GX, N_GY, N_GZ)
    coords = [device // (N_GY * N_GZ), (device // N_GZ) % N_GY, device % N_GZ]
    result = []
    for moved in (-1, 1):
        shifted = list(coords)
        shifted[axis_id] = (coords[axis_id] + moved) % extent[axis_id]
        result.append((shifted[0] * N_GY + shifted[1]) * N_GZ + shifted[2])
    return result


def reference(positions, features, species, species_embed, w_charge, wave_vectors, wave_filter, radial_decay, w_edge, w_out, neighbour_index, edge_count, edge_length, face_rows, cotangent):
    devices = N_GX * N_GY * N_GZ
    scaling = ATOMS ** -0.5
    charges = jnp.dot(features, w_charge, precision=highest) + species_embed[species]
    position_blocks = positions.reshape(3, devices, A_DEV).transpose(1, 0, 2)
    charge_blocks = charges.reshape(devices, A_DEV, C)
    feature_blocks = features.reshape(devices, A_DEV, C)
    face_blocks = face_rows.reshape(devices, 6, HALO)
    index_blocks = neighbour_index.reshape(devices, A_DEV, MAXNB)
    count_blocks = edge_count.reshape(devices, A_DEV)
    length_blocks = edge_length.reshape(devices, A_DEV, MAXNB)
    cot_blocks = cotangent.reshape(devices, A_DEV, C)
    device_ids = jnp.arange(devices, dtype=jnp.int32)

    def sum_device(running, device):
        cosines, sines = trig_tables(wave_vectors, position_blocks[device])
        term = jnp.stack([jnp.dot(cosines, charge_blocks[device], precision=highest), jnp.dot(sines, charge_blocks[device], precision=highest)])
        return running + term, None

    structure = lax.scan(sum_device, jnp.zeros((2, K, C), jnp.float32), device_ids)[0] * scaling
    filtered = wave_filter[None] * structure

    def extended_rows(device):
        blocks = [feature_blocks[device]]
        for axis_id in range(3):
            lower, upper = neighbours(device, axis_id)
            blocks.append(feature_blocks[lower][face_blocks[lower, 2 * axis_id + 1]])
            blocks.append(feature_blocks[upper][face_blocks[upper, 2 * axis_id]])
        return jnp.concatenate(blocks, axis=0)

    def forward_device(running, device):
        cosines, sines = trig_tables(wave_vectors, position_blocks[device])
        extended = extended_rows(device)
        weights = radial(length_blocks[device], count_blocks[device], radial_decay)
        messages = jnp.sum(weights * extended[index_blocks[device]], axis=1)
        potential = contract(cosines, filtered[0]) + contract(sines, filtered[1])
        preact = jnp.dot(potential, w_out, precision=highest) + jnp.dot(messages, w_edge, precision=highest)
        gate_value = jax.nn.sigmoid(preact)
        update = preact * gate_value
        grad_preact = cot_blocks[device] * gate_value * (1.0 + preact * (1.0 - gate_value))
        grad_potential = jnp.dot(grad_preact, w_out.T, precision=highest)
        grad_message = jnp.dot(grad_preact, w_edge.T, precision=highest)
        term = jnp.stack([jnp.dot(cosines, grad_potential, precision=highest), jnp.dot(sines, grad_potential, precision=highest)])
        grad_extended = jnp.zeros((extended.shape[0], C), jnp.float32).at[index_blocks[device]].add(weights * grad_message[:, None, :])
        return running + term, (update, grad_extended)

    summed, (updates, grad_blocks) = lax.scan(forward_device, jnp.zeros((2, K, C), jnp.float32), device_ids)
    grad_structure = wave_filter[None] * summed

    def backward_device(device):
        cosines, sines = trig_tables(wave_vectors, position_blocks[device])
        grad_charges = (contract(cosines, grad_structure[0]) + contract(sines, grad_structure[1])) * scaling
        gradient = grad_blocks[device][:A_DEV] + jnp.dot(grad_charges, w_charge.T, precision=highest)
        for axis_id in range(3):
            lower, upper = neighbours(device, axis_id)
            from_lower = grad_blocks[lower][A_DEV + (2 * axis_id + 1) * HALO:A_DEV + (2 * axis_id + 2) * HALO]
            from_upper = grad_blocks[upper][A_DEV + 2 * axis_id * HALO:A_DEV + (2 * axis_id + 1) * HALO]
            gradient = gradient.at[face_blocks[device, 2 * axis_id]].add(from_lower)
            gradient = gradient.at[face_blocks[device, 2 * axis_id + 1]].add(from_upper)
        return gradient

    gradients = lax.map(backward_device, device_ids)
    return updates.reshape(ATOMS, C), gradients.reshape(ATOMS, C)
```

```python
import functools
import math

import jax
import jax.numpy as jnp
from jax import lax
from jax.experimental import pallas as pl
from jax.experimental.pallas import tpu as pltpu
from jax.sharding import PartitionSpec as P

f32, bf16 = jnp.float32, jnp.bfloat16
MESH = pl.DeviceIdType.MESH
AXES = ("gx", "gy", "gz")
NX, NY, NZ = 4, 4, 16
XY = NX * NY
ZC = NZ // 2
A = 512
C = 128
KH = 512
ROWS = 2 * KH
PART = ROWS // XY
GROUP = ROWS // NX
HALO = 64
EXT = A + 6 * HALO
NB = 16
SPECIES = 89
CUTOFF = 5.0
SCALE = float((A * NX * NY * NZ) ** -0.5)
LOG2E = math.log2(math.e)
MAGIC = 12582912.0
SIN = (6.2831828185508565, -41.34142139866063, 81.59618387211225, -76.5801005149952, 41.20539481223465, -12.271262263060988)
COS = (0.9999999891722592, -19.739204532088973, 64.93911898363098, -85.45016554576007, 60.16783169583647, -25.968313174868474, 6.529610245007803)
ORDER = (2, 1, 3, 0)


def split(x):
    hi = x.astype(bf16)
    return hi, (x - hi.astype(f32)).astype(bf16)


def pair(x, axis=1):
    return jnp.concatenate(split(x), axis=axis)


def dot(a, b, dims=((1,), (0,))):
    return lax.dot_general(a, b, (dims, ((), ())), preferred_element_type=f32)


def fold(r):
    return r[:, :C] + r[:, C:]


def dot3(a_hi, a_lo, b_pair):
    return fold(dot(a_hi, b_pair)) + dot(a_lo, b_pair[:, :C])


def mm3(a, b):
    return dot3(*split(a), pair(b))


def mm3_nt(a, b):
    hi, lo = split(a)
    b_pair = pair(b, 0)
    r = dot(hi, b_pair, ((1,), (1,)))
    n = b.shape[0]
    return r[:, :n] + r[:, n:] + dot(lo, b_pair[:n], ((1,), (1,)))


def turns(ph):
    r = ph - ((ph + MAGIC) - MAGIC)
    u = r * r
    s, c = jnp.full_like(u, SIN[-1]), jnp.full_like(u, COS[-1])
    for k in SIN[-2::-1]:
        s = s * u + k
    for k in COS[-2::-1]:
        c = c * u + k
    return c, s * r


def kernel(
    pos_ref, feat_ref, spec_ref, emb_ref, wch_ref, wave_ref, filt_ref, decay_ref, wedge_ref, wout_ref,
    idx_ref, cnt_ref, len_ref, face_ref, cot_ref,
    upd_ref, grad_ref,
    pos_own, pos_in, q, pst, wst, wstt, ph, thi, tlo, tthi, ttlo,
    struct, rs, zs, zb, full, pacc, pout, pin, gp, back, rs2, zs2, zb2, full2, pacc2, pout2, pin2,
    emb_pad, facerow, oface, feat_t, extt, halo_out, halo_in, back_out, back_in,
    idx_t, len_t, env_t, dec_t, rad, msg, msgw, gmt, ge, gmain,
    send, recv, group_recv,
):
    gx, gy, gz = (lax.axis_index(a) for a in AXES)
    core = lax.rem(gz, 2)
    xy = gx * NY + gy
    partner = (gx, gy, gz + 1 - 2 * core)

    def shifted(dx, dy, dz):
        return (lax.rem(gx + dx, NX), lax.rem(gy + dy, NY), lax.rem(gz + dz, NZ))

    far_z = (gx, gy, lax.rem(gz + NZ - 1 + 2 * core, NZ))
    peers = [shifted(dx, dy, 0) for dx in range(NX) for dy in range(NY) if dx or dy]
    peers += [shifted(0, 0, 2 * dz) for dz in range(1, ZC)]
    peers += [partner, far_z]
    barrier = pltpu.get_barrier_semaphore()
    for peer in peers:
        pl.semaphore_signal(barrier, inc=1, device_id=peer, device_id_type=MESH)

    def copy(src, dst, send_id, recv_sem, device):
        return pltpu.make_async_remote_copy(
            src_ref=src, dst_ref=dst, send_sem=send.at[send_id], recv_sem=recv_sem, device_id=device, device_id_type=MESH
        )

    def arrived(ref, sem):
        copy(ref, ref, 0, sem, partner).wait_recv()

    def left(ref, send_id):
        copy(ref, ref, send_id, recv.at[0], partner).wait_send()

    feat = feat_ref[...]
    emb_pad[...] = jnp.zeros_like(emb_pad)
    emb_pad[0:SPECIES, :] = emb_ref[...]
    of_species = (lax.broadcasted_iota(jnp.int32, (C, A), 0) == spec_ref[...]).astype(f32).astype(bf16)
    q[0] = mm3(feat, wch_ref[...]) + fold(dot(of_species, pair(emb_pad[...]), ((0,), (0,))))

    def parts(x):
        p1 = x.astype(bf16).astype(f32)
        p2 = (x - p1).astype(bf16).astype(f32)
        return p1, p2, ((x - p1) - p2).astype(bf16).astype(f32)

    pos_own[...] = jnp.zeros_like(pos_own)
    pos_own[0:3, :] = pos_ref[...] * (1.0 / (2.0 * math.pi))
    wst[...] = jnp.zeros_like(wst)
    wparts = parts(wave_ref[:, pl.ds(pl.multiple_of(core * KH, KH), KH)])
    for i, k in enumerate((0, 0, 1, 1, 0, 2)):
        wst[8 * i : 8 * i + 3, :] = wparts[k]
    wstt[...] = wst[...].T

    def set_positions(half, value):
        pparts = parts(value)
        for i, k in enumerate((0, 1, 0, 1, 2, 0)):
            pst[8 * i : 8 * i + 8, A * half : A * half + A] = pparts[k]

    def tables(g, half):
        cols = slice(A * half, A * half + A)
        krow = pl.multiple_of(g * (GROUP // 2), GROUP // 2)
        ph[...] = dot(wstt[pl.ds(krow, GROUP // 2), :].astype(bf16), pst[:, cols].astype(bf16))
        row = pl.multiple_of(g * GROUP, GROUP)
        for i in range(4):
            c, s = turns(ph[32 * i : 32 * i + 32, :])
            for j, x in enumerate((c, s)):
                hi, lo = split(x)
                at = pl.ds(row + 64 * i + 32 * j, 32)
                thi[at, cols] = hi
                tlo[at, cols] = lo

    set_positions(0, pos_own[...])

    def own_tables(g, _):
        tables(g, 0)
        return 0

    lax.fori_loop(0, NX, own_tables, 0)

    pl.semaphore_wait(barrier, len(peers))
    copy(q.at[0], q.at[1], 0, recv.at[0], partner).start()
    copy(pos_own, pos_in, 1, recv.at[1], partner).start()

    for i in range(6):
        facerow[0:1, HALO * i : HALO * i + HALO] = face_ref[i : i + 1, :]
    oface[...] = (lax.broadcasted_iota(jnp.int32, (A, 6 * HALO), 0) == facerow[0:1, :]).astype(f32).astype(bf16)
    halo_out[...] = fold(dot(oface[...], pair(feat), ((0,), (0,))))

    def exchange_faces(src, dst, send_id, recv_id, slot):
        for t, (lower, upper) in enumerate((
            (shifted(NX - 1, 0, 0), shifted(1, 0, 0)),
            (shifted(0, NY - 1, 0), shifted(0, 1, 0)),
            (shifted(0, 0, NZ - 1), shifted(0, 0, 1)),
        )):
            for side, device in ((0, lower), (1, upper)):
                out, there = 2 * t + side, 2 * t + 1 - side
                copy(
                    src.at[pl.ds(slot + HALO * out, HALO)], dst.at[pl.ds(HALO * there, HALO)], send_id, recv.at[recv_id], device
                ).start()

    exchange_faces(halo_out, halo_in, 2, 2, 0)

    arrived(pos_in, recv.at[1])
    set_positions(1, pos_in[...])
    arrived(q.at[1], recv.at[0])
    q_pair = jnp.concatenate([pair(q[0]), pair(q[1])], axis=0)

    def rows(g):
        return pl.ds(pl.multiple_of(g * GROUP, GROUP), GROUP)

    def scatter_group(dx, src, dst, send_id, recv_id):
        for dy in ORDER:
            if dx or dy:
                device = shifted(dx, dy, 0)
                p = device[0] * NY + device[1]
                copy(
                    src.at[pl.ds(pl.multiple_of(p * PART, PART), PART)], dst.at[dx * NY + dy], send_id, recv.at[recv_id], device
                ).start()

    for dx in ORDER:
        g = lax.rem(gx + dx, NX)
        tables(g, 1)
        struct[rows(g), :] = dot3(thi[rows(g), :], tlo[rows(g), :], q_pair)
        scatter_group(dx, struct, rs, 3, 3)

    def mine(src):
        return src[pl.ds(pl.multiple_of(xy * PART, PART), PART), :]

    def along_z(total, zs, zb, send_id, recv_id):
        zs[...] = total
        for dz in (4, 3, 5, 2, 6, 1, 7):
            copy(zs, zb.at[dz], send_id, recv.at[recv_id], shifted(0, 0, 2 * dz)).start()

    def gather_parts(value, full, send_id, sems):
        own = full.at[pl.ds(pl.multiple_of(xy * PART, PART), PART)]
        own[...] = value
        for dx in ORDER:
            for dy in ORDER:
                if dx or dy:
                    copy(own, own, send_id, group_recv.at[sems + dx], shifted(dx, dy, 0)).start()

    def group_arrived(dx, full, sems):
        g = lax.rem(gx + NX - dx, NX)
        n = GROUP if dx else GROUP - PART
        arrived(full.at[pl.ds(0, n)], group_recv.at[sems + dx])
        return g

    def transposed(g, _):
        tthi[g] = thi[rows(g), :].T
        ttlo[g] = tlo[rows(g), :].T
        return 0

    lax.fori_loop(0, NX, transposed, 0)
    idx_t[...] = idx_ref[...].T
    length = len_ref[...].T
    len_t[...] = length
    scaled = length * (1.0 / CUTOFF)
    envelope = 1.0 - scaled * scaled
    live = lax.broadcasted_iota(jnp.int32, (NB, A), 0) < cnt_ref[...]
    env_t[...] = jnp.where(live, envelope * envelope, 0.0)
    dec_t[...] = jnp.broadcast_to(decay_ref[...] * (-LOG2E), (C, C)).T
    extt[:, 0:A] = pair(feat_ref[...].T, 0)

    def one_hot(e):
        return (lax.broadcasted_iota(jnp.int32, (EXT, A), 0) == idx_t[pl.ds(e, 1), :]).astype(f32).astype(bf16)

    def gather_edge(e, _):
        got = dot(extt[...], one_hot(e))
        decay = jnp.concatenate([dec_t[...]] * 4, axis=1)
        radial = env_t[pl.ds(e, 1), :] * jnp.exp2(decay * len_t[pl.ds(e, 1), :])
        rad[e] = radial
        msg[...] += radial * (got[:C] + got[C:])
        return 0

    arrived(halo_in, recv.at[2])
    extt[:, A:EXT] = pair(halo_in[...].T, 0)
    msg[...] = jnp.zeros_like(msg)

    arrived(rs.at[pl.ds(1, XY - 1)], recv.at[3])
    total = mine(struct)
    for i in range(1, XY):
        total = total + rs[i]
    along_z(total, zs, zb, 4, 4)

    lax.fori_loop(0, NB // 2, gather_edge, 0)

    arrived(zb.at[pl.ds(1, ZC - 1)], recv.at[4])
    filt = filt_ref[pl.ds(pl.multiple_of(core * KH + xy * (PART // 2), PART // 2), PART // 2), :]
    filt = jnp.concatenate([filt, filt], axis=0) * SCALE
    total = zs[...]
    for i in range(1, ZC):
        total = total + zb[i]
    gather_parts(mm3(total * filt, wout_ref[...]), full, 5, 0)

    lax.fori_loop(NB // 2, NB, gather_edge, 0)
    msgw[...] = mm3(msg[...].T, wedge_ref[...])

    def spread_parts(full, sems, pacc, pout, pin, send_id, recv_id):
        pacc[...] = jnp.zeros_like(pacc)
        for dx in (0, 1, 3):
            g = group_arrived(dx, full, sems)
            pacc[...] += dot3(tthi[g], ttlo[g], pair(full[rows(g), :]))
        g = group_arrived(2, full, sems)
        f_pair = pair(full[rows(g), :])
        pout[...] = pacc[A:, :] + dot3(tthi[g, A:], ttlo[g, A:], f_pair)
        copy(pout, pin, send_id, recv.at[recv_id], partner).start()
        mine = pacc[:A, :] + dot3(tthi[g, :A], ttlo[g, :A], f_pair)
        arrived(pin, recv.at[recv_id])
        return mine + pin[...]

    preact = spread_parts(full, 0, pacc, pout, pin, 6, 5) + msgw[...]
    gate = jax.nn.sigmoid(preact)
    upd_ref[...] = preact * gate
    gp[0] = cot_ref[...] * gate * (1.0 + preact * (1.0 - gate))
    copy(gp.at[0], gp.at[1], 7, recv.at[6], partner).start()

    gp_pair = pair(gp[0])
    back[...] = dot3(thi[:, :A], tlo[:, :A], gp_pair)
    arrived(gp.at[1], recv.at[6])
    gp_pair = pair(gp[1])
    for dx in ORDER:
        g = lax.rem(gx + dx, NX)
        back[rows(g), :] += dot3(thi[rows(g), A:], tlo[rows(g), A:], gp_pair)
        scatter_group(dx, back, rs2, 8, 7)

    gmt[...] = mm3_nt(wedge_ref[...], gp[0])
    ge[...] = jnp.zeros_like(ge)

    def spread_edge(e, _):
        ge[...] += dot(one_hot(e), pair(rad[e] * gmt[...], 0), ((1,), (1,)))
        return 0

    lax.fori_loop(0, NB // 2, spread_edge, 0)

    arrived(rs2.at[pl.ds(1, XY - 1)], recv.at[7])
    total = mine(back)
    for i in range(1, XY):
        total = total + rs2[i]
    along_z(total, zs2, zb2, 9, 8)

    lax.fori_loop(NB // 2, NB, spread_edge, 0)
    back_out[...] = fold(ge[A:, :])
    exchange_faces(back_out, back_in, 10, 9, 0)

    arrived(zb2.at[pl.ds(1, ZC - 1)], recv.at[8])
    total = zs2[...]
    for i in range(1, ZC):
        total = total + zb2[i]
    value = mm3_nt(mm3_nt(total, wout_ref[...]) * filt, wch_ref[...])
    gather_parts(value, full2, 11, 4)

    arrived(back_in, recv.at[9])
    gmain[...] = fold(ge[:A, :]) + fold(dot(oface[...], pair(back_in[...])))
    grad_ref[...] = spread_parts(full2, 4, pacc2, pout2, pin2, 12, 10) + gmain[...]

    for ref, i in (
        (q.at[0], 0), (pos_own, 1), (halo_out, 2), (rs.at[pl.ds(1, XY - 1)], 3), (zb.at[pl.ds(1, ZC - 1)], 4),
        (rs.at[pl.ds(1, XY - 1)], 5), (pout, 6), (gp.at[0], 7), (rs.at[pl.ds(1, XY - 1)], 8), (zb.at[pl.ds(1, ZC - 1)], 9),
        (halo_out, 10), (rs.at[pl.ds(1, XY - 1)], 11), (pout, 12),
    ):
        left(ref, i)


def per_device(
    positions, features, species, species_embed, w_charge, wave_vectors, wave_filter, radial_decay, w_edge, w_out,
    neighbour_index, edge_count, edge_length, face_rows, cotangent,
):
    v = lambda *shape: pltpu.VMEM(shape, f32)
    h = lambda *shape: pltpu.VMEM(shape, bf16)
    reduction = [v(ROWS, C), v(XY, PART, C), v(PART, C), v(ZC, PART, C), v(ROWS, C), v(2 * A, C), v(A, C), v(A, C)]
    scratch = [
        v(8, A), v(8, A), v(2, A, C), v(48, 2 * A), v(48, KH), v(KH, 48), v(GROUP // 2, A),
        h(ROWS, 2 * A), h(ROWS, 2 * A), h(NX, 2 * A, GROUP), h(NX, 2 * A, GROUP),
        *reduction, v(2, A, C), *reduction,
        v(C, C), pltpu.VMEM((8, 6 * HALO), jnp.int32), h(A, 6 * HALO), v(8, C), h(2 * C, EXT),
        v(6 * HALO, C), v(6 * HALO, C), v(6 * HALO, C), v(6 * HALO, C),
        pltpu.VMEM((NB, A), jnp.int32), v(NB, A), v(NB, A), v(C, C), v(NB, C, A), v(C, A), v(A, C), v(C, A),
        v(EXT, 2 * C), v(A, C),
        pltpu.SemaphoreType.DMA((13,)), pltpu.SemaphoreType.DMA((11,)), pltpu.SemaphoreType.DMA((8,)),
    ]
    shape = jax.ShapeDtypeStruct((A, C), f32)
    vmem = pl.BlockSpec(memory_space=pltpu.VMEM)
    return pl.pallas_call(
        kernel,
        out_shape=(shape, shape),
        in_specs=[vmem] * 15,
        out_specs=(vmem, vmem),
        scratch_shapes=scratch,
        compiler_params=pltpu.CompilerParams(collective_id=0, has_side_effects=True, vmem_limit_bytes=60 << 20),
        name="block",
    )(
        positions, features, species.reshape(1, A), species_embed, w_charge, wave_vectors, wave_filter,
        radial_decay.reshape(1, C), w_edge, w_out, neighbour_index, edge_count.reshape(1, A), edge_length, face_rows, cotangent,
    )


def solution(mesh):
    atoms = P(AXES, None)
    row = P(AXES)
    in_specs = (P(None, AXES), atoms, row, P(), P(), P(), P(), P(), P(), P(), atoms, row, atoms, atoms, atoms)
    return jax.shard_map(per_device, mesh=mesh, in_specs=in_specs, out_specs=(atoms, atoms), check_vma=False)
```
